256 devices in a mesh: gz: 32 (over z_hi, y, core), gx: 8 (over x, z_lo).
Axes of the slice: x: 4, y: 4, z: 8 (z_hi: 4, z_lo: 2; z = z_hi * 2 + z_lo), core: 2. Of those that a mesh axis runs over, the one named last changes fastest.
Arguments:
- density: float32 [4096, 4096], P('gz', 'gx'), may hold values from -6 to 6
- ztaps: float32 [32, 512], replicated, may hold values from -0.25 to 0.25
- xtaps: float32 [32, 256], replicated, may hold values from -0.0625 to 0.0625
Outputs:
- wake: float32 [4096, 4096], P('gz', 'gx')
The draws below stay inside these ranges and needn't reach their ends.
All inputs are finite; a program needn't handle non-finite values.
Results may differ from the reference program's by a relative error of at most 0.0001.
Values sent between devices are 32-bit elements; how exact they have to be, the bound alone decides.
A program may use at most 192 MiB of HBM per device.

```python
import jax
import jax.numpy as jnp
from jax import lax

C = 32
TZ = 512
TX = 256
NZ = 4096
NX = 4096


def steps_of(own_key, extent, cuts, smallest, largest):
    gain = 1.0
    for dim, blocks in cuts:
        steps = jax.random.uniform(jax.random.fold_in(jax.random.fold_in(own_key, 6), dim), (blocks,), jnp.float32, smallest / len(cuts), largest / len(cuts))
        gain = gain * jnp.repeat(jnp.exp(steps), extent[dim] // blocks).reshape((-1,) + (1,) * (len(extent) - 1 - dim))
    return gain


def scatter_about(stream_key, extent, deviation, bound, pieces=(), held_as=jnp.bfloat16):
    factor_of = steps_of(stream_key, extent, pieces, -0.22, 0.18) if pieces else 1.0
    drawn = jax.random.normal(stream_key, extent, jnp.float32) * deviation * factor_of
    return jnp.minimum(jnp.maximum(drawn, -bound), bound).astype(held_as)


def setup_inputs(seed: int = 0) -> dict:
    arg_keys = jax.random.split(jax.random.key(seed), 4)
    return {
        "density": scatter_about(arg_keys[0], (NZ, NX), 1.0, 6.0, ((0, 32), (1, 8)), jnp.float32),
        "ztaps": scatter_about(arg_keys[1], (C, TZ), TZ ** -0.5, 0.25, (), jnp.float32),
        "xtaps": scatter_about(arg_keys[2], (C, TX), (TX * C) ** -0.5, 0.0625, (), jnp.float32),
    }


def along_bunch(density, taps):
    length = NZ + TZ
    kernel = jnp.zeros((length,), jnp.float32).at[:TZ].set(taps[::-1])
    spectrum = jnp.fft.rfft(density, n=length, axis=0) * jnp.fft.rfft(kernel)[:, None]
    return jnp.fft.irfft(spectrum, n=length, axis=0)[TZ - 1:TZ - 1 + NZ]


def across_bunch(partial_value, taps):
    length = NX + TX
    kernel = jnp.zeros((length,), jnp.float32).at[:TX].set(taps[::-1])
    spectrum = jnp.fft.rfft(partial_value, n=length, axis=1) * jnp.fft.rfft(kernel)[None, :]
    offset = TX - 1 - TX // 2
    return jnp.fft.irfft(spectrum, n=length, axis=1)[:, offset:offset + NX]


def reference(density, ztaps, xtaps):
    def channel_term(position, running):
        partial_value = along_bunch(density, ztaps[position])
        return running + across_bunch(partial_value, xtaps[position])

    return lax.fori_loop(0, C, channel_term, jnp.zeros((NZ, NX), jnp.float32))
```

```python
import jax
import jax.numpy as jnp
import ml_dtypes
import numpy as np
from jax import lax
from jax.experimental import pallas as pl
from jax.experimental.pallas import tpu as pltpu
from jax.sharding import PartitionSpec as P

MESH = pl.DeviceIdType.MESH
F32, BF16 = jnp.float32, jnp.bfloat16
LZ, LX = 768, 512
NORM = 4.0 / (LZ * LX)


def split_np(matrix):
    high = matrix.astype(ml_dtypes.bfloat16)
    low = (matrix - high.astype(np.float64)).astype(ml_dtypes.bfloat16)
    return np.stack([high, low])


def constants():
    freq = np.arange(LZ // 2)
    angle = 2 * np.pi * np.outer(freq + 0.5, np.arange(LZ)) / LZ
    both = np.stack([np.cos(angle).reshape(3, 128, LZ), -np.sin(angle).reshape(3, 128, LZ)], axis=1)
    fz = both.reshape(LZ, LZ)
    angle = 2 * np.pi * np.outer(np.arange(LX), np.arange(LX // 2) + 0.5) / LX
    fx = np.concatenate([np.cos(angle), -np.sin(angle)], axis=1)
    return split_np(fz), split_np(fz[:, :256].T), split_np(fx[:256]), split_np(fx.T)


def dot(a, b, dims=((1,), (0,))):
    return lax.dot_general(a, b, (dims, ((), ())), preferred_element_type=F32)


def dot3(ah, al, bh, bl, dims=((1,), (0,))):
    return dot(ah, bh, dims) + dot(ah, bl, dims) + dot(al, bh, dims)


def split(value):
    high = value.astype(BF16)
    return high, (value - high.astype(F32)).astype(BF16)


def kernel(
    dens, zt_ref, xt_ref, fz_hbm, iz_hbm, fx_hbm, ix_hbm, out,
    win, fz, iz, fx, ix, acc, khat, zt, what, wake, sib, edge,
    csem, ssem, rsem, essem, ersem,
):
    gz, gx = lax.axis_index("gz"), lax.axis_index("gx")
    row, core = gz // 2, gz % 2

    def at(chip_row, which, column):
        return lax.rem((chip_row + 32) * 2 + which, 32), lax.rem(column + 8, 8)

    other = 1 - core
    barrier = pltpu.get_barrier_semaphore()
    sources = [at(row, other, gx), at(row, 1, gx - 1), at(row, 0, gx + 1)]
    for ahead in (1, 2):
        sources += [at(row + ahead, which, gx) for which in (0, 1)]
    for source in sources:
        pl.semaphore_signal(barrier, inc=1, device_id=source, device_id_type=MESH)

    loads = [
        pltpu.make_async_copy(a, b, csem.at[i])
        for i, (a, b) in enumerate([(fz_hbm, fz), (fx_hbm, fx), (iz_hbm, iz), (ix_hbm, ix)])
    ]
    for load in loads:
        load.start()
    mine = pltpu.make_async_copy(
        dens.at[:, pl.ds(pl.multiple_of(core * 256, 256), 256)],
        win.at[pl.ds(pl.multiple_of(core * 128, 128), 128)],
        csem.at[4],
    )
    mine.start()
    pl.semaphore_wait(barrier, len(sources))

    def piece(behind, which, slot):
        return pltpu.make_async_remote_copy(
            src_ref=dens.at[:, pl.ds(pl.multiple_of(which * 256, 256), 256)],
            dst_ref=win.at[pl.ds(pl.multiple_of(behind * 256 + core * 128, 128), 128)],
            send_sem=ssem.at[slot],
            recv_sem=rsem.at[behind * 2 + core],
            device_id=at(row - behind, which, gx),
            device_id_type=MESH,
        )

    def arrived(ahead, which):
        here = win.at[pl.ds(pl.multiple_of(ahead * 256 + which * 128, 128), 128)]
        pltpu.make_async_remote_copy(
            src_ref=here, dst_ref=here, send_sem=ssem.at[0], recv_sem=rsem.at[ahead * 2 + which],
            device_id=at(row, other, gx), device_id_type=MESH,
        ).wait_recv()

    sends = [piece(1, 0, 0), piece(1, 1, 1), piece(2, 0, 2), piece(2, 1, 3), piece(0, other, 4)]
    for send in sends:
        send.start()

    for load in loads:
        load.wait()
    th, tl = split(zt_ref[...])
    for t in range(3):
        rows = slice(256 * t, 256 * t + 256)
        zt[rows, :] = dot3(fz[0, rows, :512], fz[1, rows, :512], th, tl, ((1,), (1,)))
    eh, el = split(xt_ref[...])
    sign = jnp.where(lax.broadcasted_iota(jnp.int32, (1, 512), 1) % 2 == 0, -NORM, NORM)
    eh, el = split(dot3(eh, el, fx[0], fx[1]) * sign)
    for t in range(3):
        rows = slice(256 * t, 256 * t + 256)
        zh, zl = split(zt[rows, :])
        khat[rows, :] = dot3(zh, zl, eh, el)

    mine.wait()
    for ahead in range(3):
        if ahead == 0:
            arrived(0, other)
        else:
            arrived(ahead, 0)
            arrived(ahead, 1)
        block = win[256 * ahead : 256 * ahead + 256, :]
        if ahead:
            block = jnp.where(row + ahead < 16, block, 0.0)
        bh, bl = split(block)
        for t in range(3):
            rows, cols = slice(256 * t, 256 * t + 256), slice(256 * ahead, 256 * ahead + 256)
            part = dot3(fz[0, rows, cols], fz[1, rows, cols], bh, bl)
            acc[rows, :] = part if ahead == 0 else acc[rows, :] + part

    for t in range(3):
        rows = slice(256 * t, 256 * t + 256)
        ah, al = split(acc[rows, :])
        d = dot3(ah, al, fx[0], fx[1])
        k = khat[rows, :]
        d0, d1, d2, d3 = d[:128, :256], d[128:, :256], d[:128, 256:], d[128:, 256:]
        k0, k1, k2, k3 = k[:128, 256:], k[128:, 256:], k[:128, :256], k[128:, :256]
        for r, c, value in (
            (0, 0, d0 * k0 + d1 * k1 - d2 * k2 - d3 * k3),
            (128, 0, d1 * k0 - d0 * k1 + d2 * k3 - d3 * k2),
            (0, 256, d0 * k2 + d2 * k0 + d1 * k3 + d3 * k1),
            (128, 256, d3 * k0 - d0 * k3 + d1 * k2 - d2 * k1),
        ):
            high, low = split(value)
            what[0, 256 * t + r : 256 * t + r + 128, c : c + 256] = high
            what[1, 256 * t + r : 256 * t + r + 128, c : c + 256] = low

    yh, yl = split(dot3(iz[0], iz[1], what[0], what[1]))
    wake[...] = dot3(yh, yl, ix[0], ix[1])

    own_from, own_to = pl.multiple_of(128 * other, 128), pl.multiple_of(128 * core, 128)
    step = 2 * core - 1
    gives = [
        pltpu.make_async_remote_copy(
            src_ref=wake.at[pl.ds(128 * r, 128), pl.ds(pl.multiple_of(384 * core, 128), 128)],
            dst_ref=edge.at[other], send_sem=essem.at[r], recv_sem=ersem.at[other],
            device_id=at(row, r, gx + step), device_id_type=MESH,
        )
        for r in (0, 1)
    ]
    gives.append(
        pltpu.make_async_remote_copy(
            src_ref=wake.at[pl.ds(pl.multiple_of(128 * other, 128), 128), pl.ds(own_from, 384)],
            dst_ref=sib, send_sem=essem.at[2], recv_sem=ersem.at[2],
            device_id=at(row, other, gx), device_id_type=MESH,
        )
    )
    for give in gives:
        give.start()
    rows = pl.ds(pl.multiple_of(128 * core, 128), 128)
    out[:, pl.ds(pl.multiple_of(384 * other, 128), 128)] = jnp.zeros((128, 128), F32)
    out[:, pl.ds(own_to, 384)] = wake[rows, pl.ds(own_from, 384)]
    gives[2].wait_recv()
    their = pl.ds(pl.multiple_of(128 * other, 128), 384)
    out[:, their] = out[:, their] + sib[...]
    for side in (0, 1):
        here = edge.at[side]
        pltpu.make_async_remote_copy(
            src_ref=here, dst_ref=here, send_sem=essem.at[0], recv_sem=ersem.at[side],
            device_id=at(row, other, gx), device_id_type=MESH,
        ).wait_recv()
        there = slice(0, 128) if side == 0 else slice(384, 512)
        inside = gx > 0 if side == 0 else gx < 7
        out[:, there] = out[:, there] + jnp.where(inside, edge[side], 0.0)
    for copy in sends + gives:
        copy.wait_send()


def local(mats, density, ztaps, xtaps):
    any_, vmem = pl.BlockSpec(memory_space=pl.ANY), pl.BlockSpec(memory_space=pltpu.VMEM)
    return pl.pallas_call(
        kernel,
        out_shape=jax.ShapeDtypeStruct(density.shape, F32),
        in_specs=[any_, vmem, vmem] + [any_] * 4,
        out_specs=vmem,
        scratch_shapes=[
            pltpu.VMEM((LZ, 256), F32),
            *[pltpu.VMEM(m.shape, BF16) for m in mats],
            pltpu.VMEM((LZ, 256), F32),
            pltpu.VMEM((LZ, LX), F32),
            pltpu.VMEM((LZ, 32), F32),
            pltpu.VMEM((2, LZ, LX), BF16),
            pltpu.VMEM((256, LX), F32),
            pltpu.VMEM((128, 384), F32),
            pltpu.VMEM((2, 128, 128), F32),
            pltpu.SemaphoreType.DMA((5,)),
            pltpu.SemaphoreType.DMA((5,)),
            pltpu.SemaphoreType.DMA((6,)),
            pltpu.SemaphoreType.DMA((3,)),
            pltpu.SemaphoreType.DMA((3,)),
        ],
        compiler_params=pltpu.CompilerParams(
            collective_id=0, has_side_effects=True, vmem_limit_bytes=48 * 2**20
        ),
    )(density, ztaps, xtaps, *mats)


def solution(mesh):
    mats = [jnp.asarray(m) for m in constants()]
    return jax.shard_map(
        lambda *args: local(mats, *args),
        mesh=mesh,
        in_specs=(P("gz", "gx"), P(), P()),
        out_specs=P("gz", "gx"),
        check_vma=False,
    )
```

```python
import jax
import jax.numpy as jnp
import ml_dtypes
import numpy as np
from jax import lax
from jax.experimental import pallas as pl
from jax.experimental.pallas import tpu as pltpu
from jax.sharding import PartitionSpec as P

MESH = pl.DeviceIdType.MESH
F32, BF16 = jnp.float32, jnp.bfloat16
LZ, LX = 768, 512
CUT = 48
NORM = 4.0 / (LZ * LX)


def split_np(matrix):
    high = matrix.astype(ml_dtypes.bfloat16)
    low = (matrix - high.astype(np.float64)).astype(ml_dtypes.bfloat16)
    return np.stack([high, low])


def constants():
    freq = np.arange(LZ // 2)
    angle = 2 * np.pi * np.outer(freq + 0.5, np.arange(LZ)) / LZ
    both = np.stack([np.cos(angle).reshape(3, 128, LZ), -np.sin(angle).reshape(3, 128, LZ)], axis=1)
    fz = both.reshape(LZ, LZ)
    angle = 2 * np.pi * np.outer(np.arange(LX), np.arange(LX // 2) + 0.5) / LX
    fx = np.concatenate([np.cos(angle), -np.sin(angle)], axis=1)
    return split_np(fz), split_np(fz[:, :256].T), split_np(fx[:256]), split_np(fx.T)


def dot(a, b, dims=((1,), (0,))):
    return lax.dot_general(a, b, (dims, ((), ())), preferred_element_type=F32)


def dot3(ah, al, bh, bl, dims=((1,), (0,))):
    return dot(ah, bh, dims) + dot(ah, bl, dims) + dot(al, bh, dims)


def split(value):
    high = value.astype(BF16)
    return high, (value - high.astype(F32)).astype(BF16)


def kernel(
    dens, zt_hbm, xt_hbm, fz_hbm, iz_hbm, fx_hbm, ix_hbm, out,
    win, up_in, turn_in, zt_ref, xt_ref, fz, iz, fx, ix, acc, khat, zt, what, wake, sib, edge,
    csem, ssem, rsem, essem, ersem,
):
    gz, gx = lax.axis_index("gz"), lax.axis_index("gx")
    row, core = gz // 2, gz % 2

    def at(chip_row, which, column):
        return lax.rem((chip_row + 32) * 2 + which, 32), lax.rem(column + 8, 8)

    def along_y(chip_row, by):
        chip_row = lax.rem(chip_row + 32, 16)
        return chip_row // 4 * 4 + lax.rem(chip_row + 4 + by, 4)

    other, last, first = 1 - core, row % 4 == 3, row % 4 == 0
    barrier = pltpu.get_barrier_semaphore()
    sources = [at(row, other, gx), at(row, 1, gx - 1), at(row, 0, gx + 1)]
    sources += [at(along_y(row + 2, 1), core, gx), at(row + 4, core, gx)]
    for which in (0, 1):
        sources += [at(row + 1, which, gx), at(along_y(row, 1), which, gx), at(along_y(row, -1), which, gx)]
    for source in sources:
        pl.semaphore_signal(barrier, inc=1, device_id=source, device_id_type=MESH)

    loads = [
        pltpu.make_async_copy(a, b, csem.at[i])
        for i, (a, b) in enumerate([(zt_hbm, zt_ref), (xt_hbm, xt_ref), (fz_hbm, fz), (fx_hbm, fx), (iz_hbm, iz), (ix_hbm, ix)])
    ]
    for load in loads:
        load.start()
    mine = pltpu.make_async_copy(
        dens.at[:, pl.ds(pl.multiple_of(core * 256, 256), 256)],
        win.at[pl.ds(pl.multiple_of(core * 128, 128), 128)],
        csem.at[6],
    )
    mine.start()
    pl.semaphore_wait(barrier, len(sources))

    def half(which, start, stop):
        return dens.at[start:stop, pl.ds(pl.multiple_of(which * 256, 256), 256)]

    def rows_of(ahead, which, start, stop):
        return win.at[pl.ds(pl.multiple_of(ahead * 256 + which * 128 + start, 16), stop - start)]

    def send(source, there, slot, landing, device):
        return pltpu.make_async_remote_copy(
            src_ref=source, dst_ref=there, send_sem=ssem.at[slot], recv_sem=rsem.at[landing],
            device_id=device, device_id_type=MESH,
        )

    def arrived(here, landing):
        send(here, here, 0, landing, at(row, other, gx)).wait_recv()

    sends = []
    for which in (0, 1):
        near = send(half(which, 0, CUT), rows_of(1, core, 0, CUT), which, core, at(row - 1, which, gx))
        up = send(half(which, CUT, 128), up_in.at[core], 4 + which, 8 + core, at(along_y(row, 1), which, gx))
        far = send(half(which, CUT, 128), rows_of(1, core, CUT, 128), 2 + which, 2 + core, at(row - 1, which, gx))
        turn = send(half(which, CUT, 128), turn_in.at[core], 2 + which, 10 + core, at(along_y(row, -1), which, gx))
        up.start()
        pl.when(first)(turn.start)
        pl.when(jnp.logical_not(first))(far.start)
        near.start()
        sends += [near, up, far]
    sib_send = send(half(other, 0, 128), rows_of(0, core, 0, 128), 6, 12, at(row, other, gx))
    sib_send.start()
    sends.append(sib_send)

    def relays():
        passed, turned = [], []
        for which in (0, 1):
            arrived(up_in.at[which], 8 + which)
            passed.append(
                send(up_in.at[which], rows_of(2, which, CUT, 128), 7 + which, 4 + which, at(along_y(row, -1) - 2, core, gx))
            )
            passed[-1].start()
        for which in (0, 1):
            turned.append(
                send(turn_in.at[which], rows_of(1, which, CUT, 128), 11 + which, 2 + which, at(row - 4, core, gx))
            )

        @pl.when(last)
        def _():
            for which in (0, 1):
                arrived(turn_in.at[which], 10 + which)
                turned[which].start()

        for which in (0, 1):
            arrived(rows_of(1, which, 0, CUT), which)
            passed.append(
                send(rows_of(1, which, 0, CUT), rows_of(2, which, 0, CUT), 9 + which, 6 + which, at(row - 1, core, gx))
            )
            passed[-1].start()
        return passed, turned

    for load in loads:
        load.wait()
    th, tl = split(zt_ref[...])
    for t in range(3):
        rows = slice(256 * t, 256 * t + 256)
        zt[rows, :] = dot3(fz[0, rows, :512], fz[1, rows, :512], th, tl, ((1,), (1,)))
    eh, el = split(xt_ref[...])
    sign = jnp.where(lax.broadcasted_iota(jnp.int32, (1, 512), 1) % 2 == 0, -NORM, NORM)
    eh, el = split(dot3(eh, el, fx[0], fx[1]) * sign)
    for t in range(3):
        rows = slice(256 * t, 256 * t + 256)
        zh, zl = split(zt[rows, :])
        khat[rows, :] = dot3(zh, zl, eh, el)

    mine.wait()
    passed, turned = relays()
    for ahead in range(3):
        if ahead == 0:
            arrived(rows_of(0, other, 0, 128), 12)
        for which in (0, 1):
            if ahead:
                arrived(rows_of(ahead, which, CUT, 128), 2 * ahead + which)
            if ahead == 2:
                arrived(rows_of(2, which, 0, CUT), 6 + which)
        block = win[256 * ahead : 256 * ahead + 256, :]
        if ahead:
            block = jnp.where(row + ahead < 16, block, 0.0)
        bh, bl = split(block)
        for t in range(3):
            rows, cols = slice(256 * t, 256 * t + 256), slice(256 * ahead, 256 * ahead + 256)
            part = dot3(fz[0, rows, cols], fz[1, rows, cols], bh, bl)
            acc[rows, :] = part if ahead == 0 else acc[rows, :] + part

    for t in range(3):
        rows = slice(256 * t, 256 * t + 256)
        ah, al = split(acc[rows, :])
        d = dot3(ah, al, fx[0], fx[1])
        k = khat[rows, :]
        d0, d1, d2, d3 = d[:128, :256], d[128:, :256], d[:128, 256:], d[128:, 256:]
        k0, k1, k2, k3 = k[:128, 256:], k[128:, 256:], k[:128, :256], k[128:, :256]
        for r, c, value in (
            (0, 0, d0 * k0 + d1 * k1 - d2 * k2 - d3 * k3),
            (128, 0, d1 * k0 - d0 * k1 + d2 * k3 - d3 * k2),
            (0, 256, d0 * k2 + d2 * k0 + d1 * k3 + d3 * k1),
            (128, 256, d3 * k0 - d0 * k3 + d1 * k2 - d2 * k1),
        ):
            high, low = split(value)
            what[0, 256 * t + r : 256 * t + r + 128, c : c + 256] = high
            what[1, 256 * t + r : 256 * t + r + 128, c : c + 256] = low

    yh, yl = split(dot3(iz[0], iz[1], what[0], what[1]))
    wake[...] = dot3(yh, yl, ix[0], ix[1])

    own_from, own_to = pl.multiple_of(128 * other, 128), pl.multiple_of(128 * core, 128)
    step = 2 * core - 1
    gives = [
        pltpu.make_async_remote_copy(
            src_ref=wake.at[pl.ds(128 * r, 128), pl.ds(pl.multiple_of(384 * core, 128), 128)],
            dst_ref=edge.at[other], send_sem=essem.at[r], recv_sem=ersem.at[other],
            device_id=at(row, r, gx + step), device_id_type=MESH,
        )
        for r in (0, 1)
    ]
    gives.append(
        pltpu.make_async_remote_copy(
            src_ref=wake.at[pl.ds(pl.multiple_of(128 * other, 128), 128), pl.ds(own_from, 384)],
            dst_ref=sib, send_sem=essem.at[2], recv_sem=ersem.at[2],
            device_id=at(row, other, gx), device_id_type=MESH,
        )
    )
    for give in gives:
        give.start()
    rows = pl.ds(pl.multiple_of(128 * core, 128), 128)
    out[:, pl.ds(pl.multiple_of(384 * other, 128), 128)] = jnp.zeros((128, 128), F32)
    out[:, pl.ds(own_to, 384)] = wake[rows, pl.ds(own_from, 384)]
    gives[2].wait_recv()
    their = pl.ds(pl.multiple_of(128 * other, 128), 384)
    out[:, their] = out[:, their] + sib[...]
    for side in (0, 1):
        here = edge.at[side]
        pltpu.make_async_remote_copy(
            src_ref=here, dst_ref=here, send_sem=essem.at[0], recv_sem=ersem.at[side],
            device_id=at(row, other, gx), device_id_type=MESH,
        ).wait_recv()
        there = slice(0, 128) if side == 0 else slice(384, 512)
        inside = gx > 0 if side == 0 else gx < 7
        out[:, there] = out[:, there] + jnp.where(inside, edge[side], 0.0)
    for copy in sends + passed + gives:
        copy.wait_send()
    for copy in turned:
        pl.when(last)(copy.wait_send)


def local(mats, density, ztaps, xtaps):
    hbm, vmem = pl.BlockSpec(memory_space=pltpu.HBM), pl.BlockSpec(memory_space=pltpu.VMEM)
    return pl.pallas_call(
        kernel,
        out_shape=jax.ShapeDtypeStruct(density.shape, F32),
        in_specs=[hbm] * 7,
        out_specs=vmem,
        scratch_shapes=[
            pltpu.VMEM((LZ, 256), F32),
            pltpu.VMEM((2, 128 - CUT, 256), F32),
            pltpu.VMEM((2, 128 - CUT, 256), F32),
            pltpu.VMEM(ztaps.shape, F32),
            pltpu.VMEM(xtaps.shape, F32),
            *[pltpu.VMEM(m.shape, BF16) for m in mats],
            pltpu.VMEM((LZ, 256), F32),
            pltpu.VMEM((LZ, LX), F32),
            pltpu.VMEM((LZ, 32), F32),
            pltpu.VMEM((2, LZ, LX), BF16),
            pltpu.VMEM((256, LX), F32),
            pltpu.VMEM((128, 384), F32),
            pltpu.VMEM((2, 128, 128), F32),
            pltpu.SemaphoreType.DMA((7,)),
            pltpu.SemaphoreType.DMA((13,)),
            pltpu.SemaphoreType.DMA((13,)),
            pltpu.SemaphoreType.DMA((3,)),
            pltpu.SemaphoreType.DMA((3,)),
        ],
        compiler_params=pltpu.CompilerParams(
            collective_id=0, has_side_effects=True, vmem_limit_bytes=56 * 2**20
        ),
    )(density, ztaps, xtaps, *mats)


def solution(mesh):
    mats = [jnp.asarray(m) for m in constants()]
    return jax.shard_map(
        lambda *args: local(mats, *args),
        mesh=mesh,
        in_specs=(P("gz", "gx"), P(), P()),
        out_specs=P("gz", "gx"),
        check_vma=False,
    )
```

```python
import functools

import jax
import jax.numpy as jnp
import ml_dtypes
import numpy as np
from jax import lax
from jax.experimental import pallas as pl
from jax.experimental.pallas import tpu as pltpu
from jax.sharding import PartitionSpec as P

MESH = pl.DeviceIdType.MESH
F32, BF16 = jnp.float32, jnp.bfloat16
LZ, LX = 768, 512
CUT = 48
NORM = 4.0 / (LZ * LX)


def split_np(matrix):
    high = matrix.astype(ml_dtypes.bfloat16)
    low = (matrix - high.astype(np.float64)).astype(ml_dtypes.bfloat16)
    return np.stack([high, low])


def constants():
    freq = np.arange(LZ // 2)
    angle = 2 * np.pi * np.outer(freq + 0.5, np.arange(LZ)) / LZ
    both = np.stack([np.cos(angle).reshape(3, 128, LZ), -np.sin(angle).reshape(3, 128, LZ)], axis=1)
    fz = both.reshape(LZ, LZ)
    angle = 2 * np.pi * np.outer(np.arange(LX), np.arange(LX // 2) + 0.5) / LX
    fx = np.concatenate([np.cos(angle), -np.sin(angle)], axis=1)
    return split_np(fz), split_np(fz[:, :256].T), split_np(fx[:256]), split_np(fx.T)


def dot(a, b, dims=((1,), (0,))):
    return lax.dot_general(a, b, (dims, ((), ())), preferred_element_type=F32)


def dot3(ah, al, bh, bl, dims=((1,), (0,))):
    return dot(ah, bh, dims) + dot(ah, bl, dims) + dot(al, bh, dims)


def split(value):
    high = value.astype(BF16)
    return high, (value - high.astype(F32)).astype(BF16)


def kernel(
    dens, zt_hbm, xt_hbm, fz_hbm, iz_hbm, fx_hbm, ix_hbm, out,
    win, up_in, turn_in, zt_ref, xt_ref, fz, iz, fx, ix, acc, khat, zt, what, wake, sib, edge,
    csem, ssem, rsem, essem, ersem,
):
    gz, gx = lax.axis_index("gz"), lax.axis_index("gx")
    row, core = gz // 2, gz % 2

    def at(chip_row, which, column):
        return lax.rem((chip_row + 32) * 2 + which, 32), lax.rem(column + 8, 8)

    def along_y(chip_row, by):
        chip_row = lax.rem(chip_row + 32, 16)
        return chip_row // 4 * 4 + lax.rem(chip_row + 4 + by, 4)

    other, last, first = 1 - core, row % 4 == 3, row % 4 == 0
    up_row, step = along_y(row, -1), 2 * core - 1
    sends_one, sends_two, passes = row >= 1, row >= 2, up_row >= 2
    gets_one, gets_two = row <= 14, row <= 13
    turns, gets_turned = last & (row > 3), last & (row <= 11)
    gives_edge = (gx + step >= 0) & (gx + step <= 7)
    barrier = pltpu.get_barrier_semaphore()

    def greet(when, *sources):
        @pl.when(when)
        def _():
            for source in sources:
                pl.semaphore_signal(barrier, inc=1, device_id=source, device_id_type=MESH)

    pl.semaphore_signal(barrier, inc=1, device_id=at(row, other, gx), device_id_type=MESH)
    greet(gets_one, *[at(row + 1, which, gx) for which in (0, 1)])
    greet(gets_two, at(along_y(row + 2, 1), core, gx))
    greet(passes, *[at(up_row, which, gx) for which in (0, 1)])
    greet(turns, *[at(along_y(row, 1), which, gx) for which in (0, 1)])
    greet(gets_turned, at(row + 4, core, gx))
    greet(gx > 0, at(row, 1, gx - 1))
    greet(gx < 7, at(row, 0, gx + 1))
    greeted = 1
    for when, number in (
        (sends_one, 2), (passes, 1), (sends_two, 2), (first & sends_one, 2), (turns, 1), (gives_edge, 2)
    ):
        greeted = greeted + jnp.where(when, number, 0)

    loads = [
        pltpu.make_async_copy(a, b, csem.at[i])
        for i, (a, b) in enumerate([(zt_hbm, zt_ref), (xt_hbm, xt_ref), (fz_hbm, fz), (fx_hbm, fx), (iz_hbm, iz), (ix_hbm, ix)])
    ]
    for load in loads:
        load.start()
    mine = pltpu.make_async_copy(
        dens.at[:, pl.ds(pl.multiple_of(core * 256, 256), 256)],
        win.at[pl.ds(pl.multiple_of(core * 128, 128), 128)],
        csem.at[6],
    )
    mine.start()
    pl.semaphore_wait(barrier, greeted)

    def half(which, start, stop):
        return dens.at[start:stop, pl.ds(pl.multiple_of(which * 256, 256), 256)]

    def rows_of(ahead, which, start, stop):
        return win.at[pl.ds(pl.multiple_of(ahead * 256 + which * 128 + start, 16), stop - start)]

    def send(source, there, slot, landing, device):
        return pltpu.make_async_remote_copy(
            src_ref=source, dst_ref=there, send_sem=ssem.at[slot], recv_sem=rsem.at[landing],
            device_id=device, device_id_type=MESH,
        )

    def arrived(here, landing):
        send(here, here, 0, landing, at(row, other, gx)).wait_recv()

    sends = []
    for which in (0, 1):
        near = send(half(which, 0, CUT), rows_of(1, core, 0, CUT), which, core, at(row - 1, which, gx))
        up = send(half(which, CUT, 128), up_in.at[core], 4 + which, 8 + core, at(along_y(row, 1), which, gx))
        far = send(half(which, CUT, 128), rows_of(1, core, CUT, 128), 2 + which, 2 + core, at(row - 1, which, gx))
        turn = send(half(which, CUT, 128), turn_in.at[core], 2 + which, 10 + core, at(along_y(row, -1), which, gx))
        pl.when(sends_two)(up.start)
        pl.when(sends_one & first)(turn.start)
        pl.when(sends_one & jnp.logical_not(first))(far.start)
        pl.when(sends_one)(near.start)
        sends += [(near, sends_one), (up, sends_two), (far, sends_one)]
    sib_send = send(half(other, 0, 128), rows_of(0, core, 0, 128), 6, 12, at(row, other, gx))
    sib_send.start()

    def relays():
        copies = []
        for which in (0, 1):
            up = send(up_in.at[which], rows_of(2, which, CUT, 128), 7 + which, 4 + which, at(up_row - 2, core, gx))
            turned = send(turn_in.at[which], rows_of(1, which, CUT, 128), 11 + which, 2 + which, at(row - 4, core, gx))
            near = send(rows_of(1, which, 0, CUT), rows_of(2, which, 0, CUT), 9 + which, 6 + which, at(row - 1, core, gx))
            copies += [(up, passes), (turned, turns), (near, sends_one & gets_one)]

        @pl.when(passes)
        def _():
            for which in (0, 1):
                arrived(up_in.at[which], 8 + which)
                copies[3 * which][0].start()

        @pl.when(turns)
        def _():
            for which in (0, 1):
                arrived(turn_in.at[which], 10 + which)
                copies[3 * which + 1][0].start()

        @pl.when(gets_one)
        def _():
            for which in (0, 1):
                arrived(rows_of(1, which, 0, CUT), which)
                pl.when(sends_one)(copies[3 * which + 2][0].start)

        return copies

    for load in loads:
        load.wait()
    th, tl = split(zt_ref[...])
    for t in range(3):
        rows = slice(256 * t, 256 * t + 256)
        zt[rows, :] = dot3(fz[0, rows, :512], fz[1, rows, :512], th, tl, ((1,), (1,)))
    eh, el = split(xt_ref[...])
    sign = jnp.where(lax.broadcasted_iota(jnp.int32, (1, 512), 1) % 2 == 0, -NORM, NORM)
    eh, el = split(dot3(eh, el, fx[0], fx[1]) * sign)
    for t in range(3):
        rows = slice(256 * t, 256 * t + 256)
        zh, zl = split(zt[rows, :])
        khat[rows, :] = dot3(zh, zl, eh, el)

    mine.wait()
    passed = relays()

    def add_block(ahead):
        if ahead == 0:
            arrived(rows_of(0, other, 0, 128), 12)
        for which in (0, 1):
            if ahead:
                arrived(rows_of(ahead, which, CUT, 128), 2 * ahead + which)
            if ahead == 2:
                arrived(rows_of(2, which, 0, CUT), 6 + which)
        bh, bl = split(win[256 * ahead : 256 * ahead + 256, :])
        for t in range(3):
            rows, cols = slice(256 * t, 256 * t + 256), slice(256 * ahead, 256 * ahead + 256)
            part = dot3(fz[0, rows, cols], fz[1, rows, cols], bh, bl)
            acc[rows, :] = part if ahead == 0 else acc[rows, :] + part

    add_block(0)
    pl.when(gets_one)(functools.partial(add_block, 1))
    pl.when(gets_two)(functools.partial(add_block, 2))

    for t in range(3):
        rows = slice(256 * t, 256 * t + 256)
        ah, al = split(acc[rows, :])
        d = dot3(ah, al, fx[0], fx[1])
        k = khat[rows, :]
        d0, d1, d2, d3 = d[:128, :256], d[128:, :256], d[:128, 256:], d[128:, 256:]
        k0, k1, k2, k3 = k[:128, 256:], k[128:, 256:], k[:128, :256], k[128:, :256]
        for r, c, value in (
            (0, 0, d0 * k0 + d1 * k1 - d2 * k2 - d3 * k3),
            (128, 0, d1 * k0 - d0 * k1 + d2 * k3 - d3 * k2),
            (0, 256, d0 * k2 + d2 * k0 + d1 * k3 + d3 * k1),
            (128, 256, d3 * k0 - d0 * k3 + d1 * k2 - d2 * k1),
        ):
            high, low = split(value)
            what[0, 256 * t + r : 256 * t + r + 128, c : c + 256] = high
            what[1, 256 * t + r : 256 * t + r + 128, c : c + 256] = low

    yh, yl = split(dot3(iz[0], iz[1], what[0], what[1]))
    wake[...] = dot3(yh, yl, ix[0], ix[1])

    own_from, own_to = pl.multiple_of(128 * other, 128), pl.multiple_of(128 * core, 128)
    gives = [
        pltpu.make_async_remote_copy(
            src_ref=wake.at[pl.ds(128 * r, 128), pl.ds(pl.multiple_of(384 * core, 128), 128)],
            dst_ref=edge.at[other], send_sem=essem.at[r], recv_sem=ersem.at[other],
            device_id=at(row, r, gx + step), device_id_type=MESH,
        )
        for r in (0, 1)
    ]
    gives = [(give, gives_edge) for give in gives]
    across = (
        pltpu.make_async_remote_copy(
            src_ref=wake.at[pl.ds(pl.multiple_of(128 * other, 128), 128), pl.ds(own_from, 384)],
            dst_ref=sib, send_sem=essem.at[2], recv_sem=ersem.at[2],
            device_id=at(row, other, gx), device_id_type=MESH,
        )
    )
    for give, when in gives:
        pl.when(when)(give.start)
    across.start()
    rows = pl.ds(pl.multiple_of(128 * core, 128), 128)
    out[:, pl.ds(pl.multiple_of(384 * other, 128), 128)] = jnp.zeros((128, 128), F32)
    out[:, pl.ds(own_to, 384)] = wake[rows, pl.ds(own_from, 384)]
    across.wait_recv()
    their = pl.ds(pl.multiple_of(128 * other, 128), 384)
    out[:, their] = out[:, their] + sib[...]

    def add_edge(side):
        here = edge.at[side]
        pltpu.make_async_remote_copy(
            src_ref=here, dst_ref=here, send_sem=essem.at[0], recv_sem=ersem.at[side],
            device_id=at(row, other, gx), device_id_type=MESH,
        ).wait_recv()
        there = slice(0, 128) if side == 0 else slice(384, 512)
        out[:, there] = out[:, there] + edge[side]

    pl.when(gx > 0)(functools.partial(add_edge, 0))
    pl.when(gx < 7)(functools.partial(add_edge, 1))
    sib_send.wait_send()
    across.wait_send()
    for copy, when in sends + passed + gives:
        pl.when(when)(copy.wait_send)


def local(mats, density, ztaps, xtaps):
    hbm, vmem = pl.BlockSpec(memory_space=pltpu.HBM), pl.BlockSpec(memory_space=pltpu.VMEM)
    return pl.pallas_call(
        kernel,
        out_shape=jax.ShapeDtypeStruct(density.shape, F32),
        in_specs=[hbm] * 7,
        out_specs=vmem,
        scratch_shapes=[
            pltpu.VMEM((LZ, 256), F32),
            pltpu.VMEM((2, 128 - CUT, 256), F32),
            pltpu.VMEM((2, 128 - CUT, 256), F32),
            pltpu.VMEM(ztaps.shape, F32),
            pltpu.VMEM(xtaps.shape, F32),
            *[pltpu.VMEM(m.shape, BF16) for m in mats],
            pltpu.VMEM((LZ, 256), F32),
            pltpu.VMEM((LZ, LX), F32),
            pltpu.VMEM((LZ, 32), F32),
            pltpu.VMEM((2, LZ, LX), BF16),
            pltpu.VMEM((256, LX), F32),
            pltpu.VMEM((128, 384), F32),
            pltpu.VMEM((2, 128, 128), F32),
            pltpu.SemaphoreType.DMA((7,)),
            pltpu.SemaphoreType.DMA((13,)),
            pltpu.SemaphoreType.DMA((13,)),
            pltpu.SemaphoreType.DMA((3,)),
            pltpu.SemaphoreType.DMA((3,)),
        ],
        compiler_params=pltpu.CompilerParams(
            collective_id=0, has_side_effects=True, vmem_limit_bytes=56 * 2**20
        ),
    )(density, ztaps, xtaps, *mats)


def solution(mesh):
    mats = [jnp.asarray(m) for m in constants()]
    return jax.shard_map(
        lambda *args: local(mats, *args),
        mesh=mesh,
        in_specs=(P("gz", "gx"), P(), P()),
        out_specs=P("gz", "gx"),
        check_vma=False,
    )
```

```python
import functools

import jax
import jax.numpy as jnp
import ml_dtypes
import numpy as np
from jax import lax
from jax.experimental import pallas as pl
from jax.experimental.pallas import tpu as pltpu
from jax.sharding import PartitionSpec as P

MESH = pl.DeviceIdType.MESH
F32, BF16 = jnp.float32, jnp.bfloat16
LZ, LX = 768, 512
CUT = 64
PARTS = 1
NORM = 4.0 / (LZ * LX)


def split_np(matrix):
    high = matrix.astype(ml_dtypes.bfloat16)
    low = (matrix - high.astype(np.float64)).astype(ml_dtypes.bfloat16)
    return np.stack([high, low])


def constants():
    freq = np.arange(LZ // 2)
    angle = 2 * np.pi * np.outer(freq + 0.5, np.arange(LZ)) / LZ
    both = np.stack([np.cos(angle).reshape(3, 128, LZ), -np.sin(angle).reshape(3, 128, LZ)], axis=1)
    fz = both.reshape(LZ, LZ)
    angle = 2 * np.pi * np.outer(np.arange(LX), np.arange(LX // 2) + 0.5) / LX
    fx = np.concatenate([np.cos(angle), -np.sin(angle)], axis=1)
    return split_np(fz), split_np(fz[:, :256].T), split_np(fx[:256]), split_np(fx.T)


def dot(a, b, dims=((1,), (0,))):
    return lax.dot_general(a, b, (dims, ((), ())), preferred_element_type=F32)


def dot3(ah, al, bh, bl, dims=((1,), (0,))):
    return dot(ah, bh, dims) + dot(ah, bl, dims) + dot(al, bh, dims)


def split(value):
    high = value.astype(BF16)
    return high, (value - high.astype(F32)).astype(BF16)


def kernel(
    dens, zt_hbm, xt_hbm, fz_hbm, iz_hbm, fx_hbm, ix_hbm, out,
    win, up_in, turn_in, zt_ref, xt_ref, fz, iz, fx, ix, acc, khat, zt, what, wake, sib, edge,
    csem, ssem, rsem, essem, ersem,
):
    gz, gx = lax.axis_index("gz"), lax.axis_index("gx")
    row, core = gz // 2, gz % 2

    def at(chip_row, which, column):
        return lax.rem((chip_row + 32) * 2 + which, 32), lax.rem(column + 8, 8)

    def along_y(chip_row, by):
        chip_row = lax.rem(chip_row + 32, 16)
        return chip_row // 4 * 4 + lax.rem(chip_row + 4 + by, 4)

    other, last, first = 1 - core, row % 4 == 3, row % 4 == 0
    up_row, step = along_y(row, -1), 2 * core - 1
    sends_one, sends_two, passes = row >= 1, row >= 2, up_row >= 2
    gets_one, gets_two = row <= 14, row <= 13
    turns, gets_turned = last & (row > 3), last & (row <= 11)
    gives_edge = (gx + step >= 0) & (gx + step <= 7)
    barrier = pltpu.get_barrier_semaphore()

    def greet(when, *sources):
        @pl.when(when)
        def _():
            for source in sources:
                pl.semaphore_signal(barrier, inc=1, device_id=source, device_id_type=MESH)

    pl.semaphore_signal(barrier, inc=1, device_id=at(row, other, gx), device_id_type=MESH)
    greet(gets_one, *[at(row + 1, which, gx) for which in (0, 1)])
    greet(gets_two, at(along_y(row + 2, 1), core, gx))
    greet(passes, *[at(up_row, which, gx) for which in (0, 1)])
    greet(turns, *[at(along_y(row, 1), which, gx) for which in (0, 1)])
    greet(gets_turned, at(row + 4, core, gx))
    greet(gx > 0, at(row, 1, gx - 1))
    greet(gx < 7, at(row, 0, gx + 1))
    greeted = 1
    for when, number in (
        (sends_one, 2), (passes, 1), (sends_two, 2), (first & sends_one, 2), (turns, 1), (gives_edge, 2)
    ):
        greeted = greeted + jnp.where(when, number, 0)

    loads = [
        pltpu.make_async_copy(a, b, csem.at[i])
        for i, (a, b) in enumerate([(zt_hbm, zt_ref), (xt_hbm, xt_ref), (fz_hbm, fz), (fx_hbm, fx), (iz_hbm, iz), (ix_hbm, ix)])
    ]
    for load in loads:
        load.start()
    mine = pltpu.make_async_copy(
        dens.at[:, pl.ds(pl.multiple_of(core * 256, 256), 256)],
        win.at[pl.ds(pl.multiple_of(core * 128, 128), 128)],
        csem.at[6],
    )
    mine.start()
    pl.semaphore_wait(barrier, greeted)

    def half(which, start, stop):
        return dens.at[start:stop, pl.ds(pl.multiple_of(which * 256, 256), 256)]

    def rows_of(ahead, which, start, stop):
        return win.at[pl.ds(pl.multiple_of(ahead * 256 + which * 128 + start, 16), stop - start)]

    def send(source, there, slot, landing, device):
        return pltpu.make_async_remote_copy(
            src_ref=source, dst_ref=there, send_sem=ssem.at[slot], recv_sem=rsem.at[landing],
            device_id=device, device_id_type=MESH,
        )

    def arrived(here, landing):
        send(here, here, 0, landing, at(row, other, gx)).wait_recv()

    def landing(kind, which, part):
        return (kind * 2 + which) * PARTS + part

    def near_rows(part):
        return CUT // PARTS * part, CUT // PARTS * (part + 1)

    def far_rows(part):
        return tuple(CUT + (128 - CUT) // PARTS * (part + i) for i in (0, 1))

    slots = iter(range(16 * PARTS))
    sends = []
    for part in range(PARTS):
        for which in (0, 1):
            slot = next(slots)
            up = send(
                half(which, *far_rows(part)), up_in.at[core, part], next(slots), landing(4, core, part),
                at(along_y(row, 1), which, gx),
            )
            far = send(
                half(which, *far_rows(part)), rows_of(1, core, *far_rows(part)), slot, landing(1, core, part),
                at(row - 1, which, gx),
            )
            turn = send(
                half(which, *far_rows(part)), turn_in.at[core, part], slot, landing(5, core, part),
                at(along_y(row, -1), which, gx),
            )
            near = send(
                half(which, *near_rows(part)), rows_of(1, core, *near_rows(part)), next(slots), landing(0, core, part),
                at(row - 1, which, gx),
            )
            pl.when(sends_two)(up.start)
            pl.when(sends_one & first)(turn.start)
            pl.when(sends_one & jnp.logical_not(first))(far.start)
            pl.when(sends_one)(near.start)
            sends += [(near, sends_one), (up, sends_two), (far, sends_one)]
    sib_send = send(half(other, 0, 128), rows_of(0, core, 0, 128), next(slots), 12 * PARTS, at(row, other, gx))
    sib_send.start()

    def relays():
        copies = []
        for part in range(PARTS):
            ups, turneds, nears = [], [], []
            for which in (0, 1):
                ups.append(send(
                    up_in.at[which, part], rows_of(2, which, *far_rows(part)), next(slots), landing(2, which, part),
                    at(up_row - 2, core, gx),
                ))
                turneds.append(send(
                    turn_in.at[which, part], rows_of(1, which, *far_rows(part)), next(slots), landing(1, which, part),
                    at(row - 4, core, gx),
                ))
                nears.append(send(
                    rows_of(1, which, *near_rows(part)), rows_of(2, which, *near_rows(part)), next(slots),
                    landing(3, which, part), at(row - 1, core, gx),
                ))
            copies += [(c, passes) for c in ups] + [(c, turns) for c in turneds]
            copies += [(c, sends_one & gets_one) for c in nears]

            @pl.when(passes)
            def _():
                for which in (0, 1):
                    arrived(up_in.at[which, part], landing(4, which, part))
                    ups[which].start()

            @pl.when(turns)
            def _():
                for which in (0, 1):
                    arrived(turn_in.at[which, part], landing(5, which, part))
                    turneds[which].start()

            @pl.when(gets_one)
            def _():
                for which in (0, 1):
                    arrived(rows_of(1, which, *near_rows(part)), landing(0, which, part))
                    pl.when(sends_one)(nears[which].start)

        return copies

    for load in loads:
        load.wait()
    th, tl = split(zt_ref[...])
    for t in range(3):
        rows = slice(256 * t, 256 * t + 256)
        zt[rows, :] = dot3(fz[0, rows, :512], fz[1, rows, :512], th, tl, ((1,), (1,)))
    eh, el = split(xt_ref[...])
    sign = jnp.where(lax.broadcasted_iota(jnp.int32, (1, 512), 1) % 2 == 0, -NORM, NORM)
    eh, el = split(dot3(eh, el, fx[0], fx[1]) * sign)
    for t in range(3):
        rows = slice(256 * t, 256 * t + 256)
        zh, zl = split(zt[rows, :])
        khat[rows, :] = dot3(zh, zl, eh, el)

    mine.wait()
    passed = relays()

    def add_block(ahead):
        if ahead == 0:
            arrived(rows_of(0, other, 0, 128), 12 * PARTS)
        for part in range(PARTS if ahead else 0):
            for which in (0, 1):
                arrived(rows_of(ahead, which, *far_rows(part)), landing(ahead, which, part))
                if ahead == 2:
                    arrived(rows_of(2, which, *near_rows(part)), landing(3, which, part))
        bh, bl = split(win[256 * ahead : 256 * ahead + 256, :])
        for t in range(3):
            rows, cols = slice(256 * t, 256 * t + 256), slice(256 * ahead, 256 * ahead + 256)
            part = dot3(fz[0, rows, cols], fz[1, rows, cols], bh, bl)
            acc[rows, :] = part if ahead == 0 else acc[rows, :] + part

    add_block(0)
    pl.when(gets_one)(functools.partial(add_block, 1))
    pl.when(gets_two)(functools.partial(add_block, 2))

    for t in range(3):
        rows = slice(256 * t, 256 * t + 256)
        ah, al = split(acc[rows, :])
        d = dot3(ah, al, fx[0], fx[1])
        k = khat[rows, :]
        d0, d1, d2, d3 = d[:128, :256], d[128:, :256], d[:128, 256:], d[128:, 256:]
        k0, k1, k2, k3 = k[:128, 256:], k[128:, 256:], k[:128, :256], k[128:, :256]
        for r, c, value in (
            (0, 0, d0 * k0 + d1 * k1 - d2 * k2 - d3 * k3),
            (128, 0, d1 * k0 - d0 * k1 + d2 * k3 - d3 * k2),
            (0, 256, d0 * k2 + d2 * k0 + d1 * k3 + d3 * k1),
            (128, 256, d3 * k0 - d0 * k3 + d1 * k2 - d2 * k1),
        ):
            high, low = split(value)
            what[0, 256 * t + r : 256 * t + r + 128, c : c + 256] = high
            what[1, 256 * t + r : 256 * t + r + 128, c : c + 256] = low

    yh, yl = split(dot3(iz[0], iz[1], what[0], what[1]))
    wake[...] = dot3(yh, yl, ix[0], ix[1])

    own_from, own_to = pl.multiple_of(128 * other, 128), pl.multiple_of(128 * core, 128)
    gives = [
        pltpu.make_async_remote_copy(
            src_ref=wake.at[pl.ds(128 * r, 128), pl.ds(pl.multiple_of(384 * core, 128), 128)],
            dst_ref=edge.at[other], send_sem=essem.at[r], recv_sem=ersem.at[other],
            device_id=at(row, r, gx + step), device_id_type=MESH,
        )
        for r in (0, 1)
    ]
    gives = [(give, gives_edge) for give in gives]
    across = (
        pltpu.make_async_remote_copy(
            src_ref=wake.at[pl.ds(pl.multiple_of(128 * other, 128), 128), pl.ds(own_from, 384)],
            dst_ref=sib, send_sem=essem.at[2], recv_sem=ersem.at[2],
            device_id=at(row, other, gx), device_id_type=MESH,
        )
    )
    for give, when in gives:
        pl.when(when)(give.start)
    across.start()
    rows = pl.ds(pl.multiple_of(128 * core, 128), 128)
    out[:, pl.ds(pl.multiple_of(384 * other, 128), 128)] = jnp.zeros((128, 128), F32)
    out[:, pl.ds(own_to, 384)] = wake[rows, pl.ds(own_from, 384)]
    across.wait_recv()
    their = pl.ds(pl.multiple_of(128 * other, 128), 384)
    out[:, their] = out[:, their] + sib[...]

    def add_edge(side):
        here = edge.at[side]
        pltpu.make_async_remote_copy(
            src_ref=here, dst_ref=here, send_sem=essem.at[0], recv_sem=ersem.at[side],
            device_id=at(row, other, gx), device_id_type=MESH,
        ).wait_recv()
        there = slice(0, 128) if side == 0 else slice(384, 512)
        out[:, there] = out[:, there] + edge[side]

    pl.when(gx > 0)(functools.partial(add_edge, 0))
    pl.when(gx < 7)(functools.partial(add_edge, 1))
    sib_send.wait_send()
    across.wait_send()
    for copy, when in sends + passed + gives:
        pl.when(when)(copy.wait_send)


def local(mats, density, ztaps, xtaps):
    hbm, vmem = pl.BlockSpec(memory_space=pltpu.HBM), pl.BlockSpec(memory_space=pltpu.VMEM)
    return pl.pallas_call(
        kernel,
        out_shape=jax.ShapeDtypeStruct(density.shape, F32),
        in_specs=[hbm] * 7,
        out_specs=vmem,
        scratch_shapes=[
            pltpu.VMEM((LZ, 256), F32),
            pltpu.VMEM((2, PARTS, (128 - CUT) // PARTS, 256), F32),
            pltpu.VMEM((2, PARTS, (128 - CUT) // PARTS, 256), F32),
            pltpu.VMEM(ztaps.shape, F32),
            pltpu.VMEM(xtaps.shape, F32),
            *[pltpu.VMEM(m.shape, BF16) for m in mats],
            pltpu.VMEM((LZ, 256), F32),
            pltpu.VMEM((LZ, LX), F32),
            pltpu.VMEM((LZ, 32), F32),
            pltpu.VMEM((2, LZ, LX), BF16),
            pltpu.VMEM((256, LX), F32),
            pltpu.VMEM((128, 384), F32),
            pltpu.VMEM((2, 128, 128), F32),
            pltpu.SemaphoreType.DMA((7,)),
            pltpu.SemaphoreType.DMA((16 * PARTS,)),
            pltpu.SemaphoreType.DMA((12 * PARTS + 1,)),
            pltpu.SemaphoreType.DMA((3,)),
            pltpu.SemaphoreType.DMA((3,)),
        ],
        compiler_params=pltpu.CompilerParams(
            collective_id=0, has_side_effects=True, vmem_limit_bytes=56 * 2**20
        ),
    )(density, ztaps, xtaps, *mats)


def solution(mesh):
    mats = [jnp.asarray(m) for m in constants()]
    return jax.shard_map(
        lambda *args: local(mats, *args),
        mesh=mesh,
        in_specs=(P("gz", "gx"), P(), P()),
        out_specs=P("gz", "gx"),
        check_vma=False,
    )
```

```python
import functools

import jax
import jax.numpy as jnp
import ml_dtypes
import numpy as np
from jax import lax
from jax.experimental import pallas as pl
from jax.experimental.pallas import tpu as pltpu
from jax.sharding import PartitionSpec as P

MESH = pl.DeviceIdType.MESH
F32, BF16 = jnp.float32, jnp.bfloat16
LZ, LX = 768, 512
CUT = 64
PARTS = 1
NORM = 4.0 / (LZ * LX)


def split_np(matrix):
    high = matrix.astype(ml_dtypes.bfloat16)
    low = (matrix - high.astype(np.float64)).astype(ml_dtypes.bfloat16)
    return np.stack([high, low])


def constants():
    freq = np.arange(LZ // 2)
    angle = 2 * np.pi * np.outer(freq + 0.5, np.arange(LZ)) / LZ
    both = np.stack([np.cos(angle).reshape(3, 128, LZ), -np.sin(angle).reshape(3, 128, LZ)], axis=1)
    fz = both.reshape(LZ, LZ)
    angle = 2 * np.pi * np.outer(np.arange(LX), np.arange(LX // 2) + 0.5) / LX
    fx = np.concatenate([np.cos(angle), -np.sin(angle)], axis=1)
    return split_np(fz), split_np(fz[:, :256].T), split_np(fx[:256]), split_np(fx.T)


def dot(a, b, dims=((1,), (0,))):
    return lax.dot_general(a, b, (dims, ((), ())), preferred_element_type=F32)


def dot3(ah, al, bh, bl, dims=((1,), (0,))):
    axis = dims[1][0]
    return dot(jnp.concatenate([ah, ah, al], axis=1), jnp.concatenate([bh, bl, bh], axis=axis), dims)


def split(value):
    high = value.astype(BF16)
    return high, (value - high.astype(F32)).astype(BF16)


def kernel(
    dens, zt_hbm, xt_hbm, fz_hbm, iz_hbm, fx_hbm, ix_hbm, out,
    win, up_in, turn_in, zt_ref, xt_ref, fz, iz, fx, ix, acc, khat, zt, what, wake, sib, edge,
    csem, ssem, rsem, essem, ersem,
):
    gz, gx = lax.axis_index("gz"), lax.axis_index("gx")
    row, core = gz // 2, gz % 2

    def at(chip_row, which, column):
        return lax.rem((chip_row + 32) * 2 + which, 32), lax.rem(column + 8, 8)

    def along_y(chip_row, by):
        chip_row = lax.rem(chip_row + 32, 16)
        return chip_row // 4 * 4 + lax.rem(chip_row + 4 + by, 4)

    other, last, first = 1 - core, row % 4 == 3, row % 4 == 0
    up_row, step = along_y(row, -1), 2 * core - 1
    sends_one, sends_two, passes = row >= 1, row >= 2, up_row >= 2
    gets_one, gets_two = row <= 14, row <= 13
    turns, gets_turned = last & (row > 3), last & (row <= 11)
    gives_edge = (gx + step >= 0) & (gx + step <= 7)
    barrier = pltpu.get_barrier_semaphore()

    def greet(when, *sources):
        @pl.when(when)
        def _():
            for source in sources:
                pl.semaphore_signal(barrier, inc=1, device_id=source, device_id_type=MESH)

    pl.semaphore_signal(barrier, inc=1, device_id=at(row, other, gx), device_id_type=MESH)
    greet(gets_one, *[at(row + 1, which, gx) for which in (0, 1)])
    greet(gets_two, at(along_y(row + 2, 1), core, gx))
    greet(passes, *[at(up_row, which, gx) for which in (0, 1)])
    greet(turns, *[at(along_y(row, 1), which, gx) for which in (0, 1)])
    greet(gets_turned, at(row + 4, core, gx))
    greet(gx > 0, at(row, 1, gx - 1))
    greet(gx < 7, at(row, 0, gx + 1))
    greeted = 1
    for when, number in (
        (sends_one, 2), (passes, 1), (sends_two, 2), (first & sends_one, 2), (turns, 1), (gives_edge, 2)
    ):
        greeted = greeted + jnp.where(when, number, 0)

    loads = [
        pltpu.make_async_copy(a, b, csem.at[i])
        for i, (a, b) in enumerate([(zt_hbm, zt_ref), (xt_hbm, xt_ref), (fz_hbm, fz), (fx_hbm, fx), (iz_hbm, iz), (ix_hbm, ix)])
    ]
    for load in loads:
        load.start()
    mine = pltpu.make_async_copy(
        dens.at[:, pl.ds(pl.multiple_of(core * 256, 256), 256)],
        win.at[pl.ds(pl.multiple_of(core * 128, 128), 128)],
        csem.at[6],
    )
    mine.start()
    pl.semaphore_wait(barrier, greeted)

    def half(which, start, stop):
        return dens.at[start:stop, pl.ds(pl.multiple_of(which * 256, 256), 256)]

    def rows_of(ahead, which, start, stop):
        return win.at[pl.ds(pl.multiple_of(ahead * 256 + which * 128 + start, 16), stop - start)]

    def send(source, there, slot, landing, device):
        return pltpu.make_async_remote_copy(
            src_ref=source, dst_ref=there, send_sem=ssem.at[slot], recv_sem=rsem.at[landing],
            device_id=device, device_id_type=MESH,
        )

    def arrived(here, landing):
        send(here, here, 0, landing, at(row, other, gx)).wait_recv()

    def landing(kind, which, part):
        return (kind * 2 + which) * PARTS + part

    def near_rows(part):
        return CUT // PARTS * part, CUT // PARTS * (part + 1)

    def far_rows(part):
        return tuple(CUT + (128 - CUT) // PARTS * (part + i) for i in (0, 1))

    slots = iter(range(16 * PARTS))
    sends = []
    for part in range(PARTS):
        for which in (0, 1):
            slot = next(slots)
            up = send(
                half(which, *far_rows(part)), up_in.at[core, part], next(slots), landing(4, core, part),
                at(along_y(row, 1), which, gx),
            )
            far = send(
                half(which, *far_rows(part)), rows_of(1, core, *far_rows(part)), slot, landing(1, core, part),
                at(row - 1, which, gx),
            )
            turn = send(
                half(which, *far_rows(part)), turn_in.at[core, part], slot, landing(5, core, part),
                at(along_y(row, -1), which, gx),
            )
            near = send(
                half(which, *near_rows(part)), rows_of(1, core, *near_rows(part)), next(slots), landing(0, core, part),
                at(row - 1, which, gx),
            )
            pl.when(sends_two)(up.start)
            pl.when(sends_one & first)(turn.start)
            pl.when(sends_one & jnp.logical_not(first))(far.start)
            pl.when(sends_one)(near.start)
            sends += [(near, sends_one), (up, sends_two), (far, sends_one)]
    sib_send = send(half(other, 0, 128), rows_of(0, core, 0, 128), next(slots), 12 * PARTS, at(row, other, gx))
    sib_send.start()

    def relays():
        copies = []
        for part in range(PARTS):
            ups, turneds, nears = [], [], []
            for which in (0, 1):
                ups.append(send(
                    up_in.at[which, part], rows_of(2, which, *far_rows(part)), next(slots), landing(2, which, part),
                    at(up_row - 2, core, gx),
                ))
                turneds.append(send(
                    turn_in.at[which, part], rows_of(1, which, *far_rows(part)), next(slots), landing(1, which, part),
                    at(row - 4, core, gx),
                ))
                nears.append(send(
                    rows_of(1, which, *near_rows(part)), rows_of(2, which, *near_rows(part)), next(slots),
                    landing(3, which, part), at(row - 1, core, gx),
                ))
            copies += [(c, passes) for c in ups] + [(c, turns) for c in turneds]
            copies += [(c, sends_one & gets_one) for c in nears]

            @pl.when(passes)
            def _():
                for which in (0, 1):
                    arrived(up_in.at[which, part], landing(4, which, part))
                    ups[which].start()

            @pl.when(turns)
            def _():
                for which in (0, 1):
                    arrived(turn_in.at[which, part], landing(5, which, part))
                    turneds[which].start()

            @pl.when(gets_one)
            def _():
                for which in (0, 1):
                    arrived(rows_of(1, which, *near_rows(part)), landing(0, which, part))
                    pl.when(sends_one)(nears[which].start)

        return copies

    for load in loads:
        load.wait()
    th, tl = split(zt_ref[...])
    for t in range(3):
        rows = slice(256 * t, 256 * t + 256)
        zt[rows, :] = dot3(fz[0, rows, :512], fz[1, rows, :512], th, tl, ((1,), (1,)))
    eh, el = split(xt_ref[...])
    sign = jnp.where(lax.broadcasted_iota(jnp.int32, (1, 512), 1) % 2 == 0, -NORM, NORM)
    eh, el = split(dot3(eh, el, fx[0], fx[1]) * sign)
    for t in range(3):
        rows = slice(256 * t, 256 * t + 256)
        zh, zl = split(zt[rows, :])
        khat[rows, :] = dot3(zh, zl, eh, el)

    mine.wait()
    passed = relays()

    def add_block(ahead):
        if ahead == 0:
            arrived(rows_of(0, other, 0, 128), 12 * PARTS)
        for part in range(PARTS if ahead else 0):
            for which in (0, 1):
                arrived(rows_of(ahead, which, *far_rows(part)), landing(ahead, which, part))
                if ahead == 2:
                    arrived(rows_of(2, which, *near_rows(part)), landing(3, which, part))
        bh, bl = split(win[256 * ahead : 256 * ahead + 256, :])
        for t in range(3):
            rows, cols = slice(256 * t, 256 * t + 256), slice(256 * ahead, 256 * ahead + 256)
            part = dot3(fz[0, rows, cols], fz[1, rows, cols], bh, bl)
            acc[rows, :] = part if ahead == 0 else acc[rows, :] + part

    add_block(0)
    pl.when(gets_one)(functools.partial(add_block, 1))
    pl.when(gets_two)(functools.partial(add_block, 2))

    for t in range(3):
        rows = slice(256 * t, 256 * t + 256)
        ah, al = split(acc[rows, :])
        d = dot3(ah, al, fx[0], fx[1])
        k = khat[rows, :]
        d0, d1, d2, d3 = d[:128, :256], d[128:, :256], d[:128, 256:], d[128:, 256:]
        k0, k1, k2, k3 = k[:128, 256:], k[128:, 256:], k[:128, :256], k[128:, :256]
        for r, c, value in (
            (0, 0, d0 * k0 + d1 * k1 - d2 * k2 - d3 * k3),
            (128, 0, d1 * k0 - d0 * k1 + d2 * k3 - d3 * k2),
            (0, 256, d0 * k2 + d2 * k0 + d1 * k3 + d3 * k1),
            (128, 256, d3 * k0 - d0 * k3 + d1 * k2 - d2 * k1),
        ):
            high, low = split(value)
            what[0, 256 * t + r : 256 * t + r + 128, c : c + 256] = high
            what[1, 256 * t + r : 256 * t + r + 128, c : c + 256] = low

    own_from, own_to = pl.multiple_of(128 * other, 128), pl.multiple_of(128 * core, 128)
    across = pltpu.make_async_remote_copy(
        src_ref=wake.at[pl.ds(pl.multiple_of(128 * other, 128), 128), pl.ds(own_from, 384)],
        dst_ref=sib, send_sem=essem.at[2], recv_sem=ersem.at[2],
        device_id=at(row, other, gx), device_id_type=MESH,
    )
    gives = []
    for r in (0, 1):
        rows = slice(128 * r, 128 * r + 128)
        yh, yl = split(dot3(iz[0, rows, :], iz[1, rows, :], what[0], what[1]))
        wake[rows, :] = dot3(yh, yl, ix[0], ix[1])
        give = pltpu.make_async_remote_copy(
            src_ref=wake.at[pl.ds(128 * r, 128), pl.ds(pl.multiple_of(384 * core, 128), 128)],
            dst_ref=edge.at[other], send_sem=essem.at[r], recv_sem=ersem.at[other],
            device_id=at(row, r, gx + step), device_id_type=MESH,
        )
        pl.when(gives_edge)(give.start)
        pl.when(other == r)(across.start)
        gives.append((give, gives_edge))
    rows = pl.ds(pl.multiple_of(128 * core, 128), 128)
    out[:, pl.ds(pl.multiple_of(384 * other, 128), 128)] = jnp.zeros((128, 128), F32)
    out[:, pl.ds(own_to, 384)] = wake[rows, pl.ds(own_from, 384)]
    across.wait_recv()
    their = pl.ds(pl.multiple_of(128 * other, 128), 384)
    out[:, their] = out[:, their] + sib[...]

    def add_edge(side):
        here = edge.at[side]
        pltpu.make_async_remote_copy(
            src_ref=here, dst_ref=here, send_sem=essem.at[0], recv_sem=ersem.at[side],
            device_id=at(row, other, gx), device_id_type=MESH,
        ).wait_recv()
        there = slice(0, 128) if side == 0 else slice(384, 512)
        out[:, there] = out[:, there] + edge[side]

    pl.when(gx > 0)(functools.partial(add_edge, 0))
    pl.when(gx < 7)(functools.partial(add_edge, 1))
    sib_send.wait_send()
    across.wait_send()
    for copy, when in sends + passed + gives:
        pl.when(when)(copy.wait_send)


def local(mats, density, ztaps, xtaps):
    hbm, vmem = pl.BlockSpec(memory_space=pltpu.HBM), pl.BlockSpec(memory_space=pltpu.VMEM)
    return pl.pallas_call(
        kernel,
        out_shape=jax.ShapeDtypeStruct(density.shape, F32),
        in_specs=[hbm] * 7,
        out_specs=vmem,
        scratch_shapes=[
            pltpu.VMEM((LZ, 256), F32),
            pltpu.VMEM((2, PARTS, (128 - CUT) // PARTS, 256), F32),
            pltpu.VMEM((2, PARTS, (128 - CUT) // PARTS, 256), F32),
            pltpu.VMEM(ztaps.shape, F32),
            pltpu.VMEM(xtaps.shape, F32),
            *[pltpu.VMEM(m.shape, BF16) for m in mats],
            pltpu.VMEM((LZ, 256), F32),
            pltpu.VMEM((LZ, LX), F32),
            pltpu.VMEM((LZ, 32), F32),
            pltpu.VMEM((2, LZ, LX), BF16),
            pltpu.VMEM((256, LX), F32),
            pltpu.VMEM((128, 384), F32),
            pltpu.VMEM((2, 128, 128), F32),
            pltpu.SemaphoreType.DMA((7,)),
            pltpu.SemaphoreType.DMA((16 * PARTS,)),
            pltpu.SemaphoreType.DMA((12 * PARTS + 1,)),
            pltpu.SemaphoreType.DMA((3,)),
            pltpu.SemaphoreType.DMA((3,)),
        ],
        compiler_params=pltpu.CompilerParams(
            collective_id=0, has_side_effects=True, vmem_limit_bytes=56 * 2**20
        ),
    )(density, ztaps, xtaps, *mats)


def solution(mesh):
    mats = [jnp.asarray(m) for m in constants()]
    return jax.shard_map(
        lambda *args: local(mats, *args),
        mesh=mesh,
        in_specs=(P("gz", "gx"), P(), P()),
        out_specs=P("gz", "gx"),
        check_vma=False,
    )
```

```python
import functools

import jax
import jax.numpy as jnp
import ml_dtypes
import numpy as np
from jax import lax
from jax.experimental import pallas as pl
from jax.experimental.pallas import tpu as pltpu
from jax.sharding import PartitionSpec as P

MESH = pl.DeviceIdType.MESH
F32, BF16 = jnp.float32, jnp.bfloat16
LZ, LX = 768, 512
CUT = 64
TURN = 64
PARTS = 1
NORM = 4.0 / (LZ * LX)


def split_np(matrix):
    high = matrix.astype(ml_dtypes.bfloat16)
    low = (matrix - high.astype(np.float64)).astype(ml_dtypes.bfloat16)
    return np.stack([high, low])


def constants():
    freq = np.arange(LZ // 2)
    angle = 2 * np.pi * np.outer(freq + 0.5, np.arange(LZ)) / LZ
    both = np.stack([np.cos(angle).reshape(3, 128, LZ), -np.sin(angle).reshape(3, 128, LZ)], axis=1)
    fz = both.reshape(LZ, LZ)
    angle = 2 * np.pi * np.outer(np.arange(LX), np.arange(LX // 2) + 0.5) / LX
    fx = np.concatenate([np.cos(angle), -np.sin(angle)], axis=1)
    return split_np(fz), split_np(fz[:, :256].T), split_np(fx[:256]), split_np(fx.T)


def dot(a, b, dims=((1,), (0,))):
    return lax.dot_general(a, b, (dims, ((), ())), preferred_element_type=F32)


def dot3(ah, al, bh, bl, dims=((1,), (0,))):
    axis = dims[1][0]
    return dot(jnp.concatenate([ah, ah, al], axis=1), jnp.concatenate([bh, bl, bh], axis=axis), dims)


def split(value):
    high = value.astype(BF16)
    return high, (value - high.astype(F32)).astype(BF16)


def kernel(
    dens, zt_hbm, xt_hbm, fz_hbm, iz_hbm, fx_hbm, ix_hbm, out,
    win, up_in, turn_in, zt_ref, xt_ref, fz, iz, fx, ix, acc, khat, zt, what, wake, sib, edge,
    csem, ssem, rsem, essem, ersem,
):
    gz, gx = lax.axis_index("gz"), lax.axis_index("gx")
    row, core = gz // 2, gz % 2

    def at(chip_row, which, column):
        return lax.rem((chip_row + 32) * 2 + which, 32), lax.rem(column + 8, 8)

    def along_y(chip_row, by):
        chip_row = lax.rem(chip_row + 32, 16)
        return chip_row // 4 * 4 + lax.rem(chip_row + 4 + by, 4)

    other, last, first = 1 - core, row % 4 == 3, row % 4 == 0
    up_row, step = along_y(row, -1), 2 * core - 1
    sends_one, sends_two, passes = row >= 1, row >= 2, up_row >= 2
    gets_one, gets_two = row <= 14, row <= 13
    turns, gets_turned = last & (row > 3), last & (row <= 11)
    gives_edge = (gx + step >= 0) & (gx + step <= 7)
    barrier = pltpu.get_barrier_semaphore()

    def greet(when, *sources):
        @pl.when(when)
        def _():
            for source in sources:
                pl.semaphore_signal(barrier, inc=1, device_id=source, device_id_type=MESH)

    pl.semaphore_signal(barrier, inc=1, device_id=at(row, other, gx), device_id_type=MESH)
    greet(gets_one, *[at(row + 1, which, gx) for which in (0, 1)])
    greet(gets_two, at(along_y(row + 2, 1), core, gx))
    greet(passes, *[at(up_row, which, gx) for which in (0, 1)])
    greet(turns, *[at(along_y(row, 1), which, gx) for which in (0, 1)])
    greet(gets_turned, at(row + 4, core, gx))
    greet(gx > 0, at(row, 1, gx - 1))
    greet(gx < 7, at(row, 0, gx + 1))
    greeted = 1
    for when, number in (
        (sends_one, 2), (passes, 1), (sends_two, 2), (first & sends_one, 2), (turns, 1), (gives_edge, 2)
    ):
        greeted = greeted + jnp.where(when, number, 0)

    loads = [
        pltpu.make_async_copy(a, b, csem.at[i])
        for i, (a, b) in enumerate([(zt_hbm, zt_ref), (xt_hbm, xt_ref), (fz_hbm, fz), (fx_hbm, fx), (iz_hbm, iz), (ix_hbm, ix)])
    ]
    for load in loads:
        load.start()
    mine = pltpu.make_async_copy(
        dens.at[:, pl.ds(pl.multiple_of(core * 256, 256), 256)],
        win.at[pl.ds(pl.multiple_of(core * 128, 128), 128)],
        csem.at[6],
    )
    mine.start()
    pl.semaphore_wait(barrier, greeted)

    def half(which, start, stop):
        return dens.at[start:stop, pl.ds(pl.multiple_of(which * 256, 256), 256)]

    def rows_of(ahead, which, start, stop):
        return win.at[pl.ds(pl.multiple_of(ahead * 256 + which * 128 + start, 16), stop - start)]

    def send(source, there, slot, landing, device):
        return pltpu.make_async_remote_copy(
            src_ref=source, dst_ref=there, send_sem=ssem.at[slot], recv_sem=rsem.at[landing],
            device_id=device, device_id_type=MESH,
        )

    def arrived(here, landing):
        send(here, here, 0, landing, at(row, other, gx)).wait_recv()

    def landing(kind, which, part):
        return (kind * 2 + which) * PARTS + part

    near_rows, far_rows, low_rows, high_rows = (0, TURN), (TURN, 128), (0, CUT), (CUT, 128)

    slots = iter(range(16 * PARTS))
    sends = []
    for part in range(PARTS):
        for which in (0, 1):
            slot = next(slots)
            up = send(
                half(which, *high_rows), up_in.at[core, part], next(slots), landing(4, core, part),
                at(along_y(row, 1), which, gx),
            )
            far = send(
                half(which, *far_rows), rows_of(1, core, *far_rows), slot, landing(1, core, part),
                at(row - 1, which, gx),
            )
            turn = send(
                half(which, *far_rows), turn_in.at[core, part], slot, landing(5, core, part),
                at(along_y(row, -1), which, gx),
            )
            near = send(
                half(which, *near_rows), rows_of(1, core, *near_rows), next(slots), landing(0, core, part),
                at(row - 1, which, gx),
            )
            pl.when(sends_two)(up.start)
            pl.when(sends_one & first)(turn.start)
            pl.when(sends_one & jnp.logical_not(first))(far.start)
            pl.when(sends_one)(near.start)
            sends += [(near, sends_one), (up, sends_two), (far, sends_one)]
    sib_send = send(half(other, 0, 128), rows_of(0, core, 0, 128), next(slots), 12 * PARTS, at(row, other, gx))
    sib_send.start()

    def relays():
        copies, steps = [], []
        for part in range(PARTS):
            ups, turneds, nears = [], [], []
            for which in (0, 1):
                ups.append(send(
                    up_in.at[which, part], rows_of(2, which, *high_rows), next(slots), landing(2, which, part),
                    at(up_row - 2, core, gx),
                ))
                turneds.append(send(
                    turn_in.at[which, part], rows_of(1, which, *far_rows), next(slots), landing(1, which, part),
                    at(row - 4, core, gx),
                ))
                nears.append(send(
                    rows_of(1, which, *low_rows), rows_of(2, which, *low_rows), next(slots),
                    landing(3, which, part), at(row - 1, core, gx),
                ))
            copies += [(c, passes) for c in ups] + [(c, turns) for c in turneds]
            copies += [(c, sends_one & gets_one) for c in nears]

            def relay_passes():
                for which in (0, 1):
                    arrived(up_in.at[which, part], landing(4, which, part))
                    ups[which].start()

            def relay_turns():
                for which in (0, 1):
                    arrived(turn_in.at[which, part], landing(5, which, part))
                    turneds[which].start()

            def relay_gets_one():
                for which in (0, 1):
                    arrived(rows_of(1, which, *near_rows), landing(0, which, part))
                    pl.when(sends_one)(nears[which].start)

            steps += [(passes, relay_passes), (turns, relay_turns), (gets_one, relay_gets_one)]
        return copies, steps

    passed, steps = relays()
    relays_first = row >= 4
    for when, relay in steps:
        pl.when(relays_first & when)(relay)

    for load in loads:
        load.wait()
    th, tl = split(zt_ref[...])
    for t in range(3):
        rows = slice(256 * t, 256 * t + 256)
        zt[rows, :] = dot3(fz[0, rows, :512], fz[1, rows, :512], th, tl, ((1,), (1,)))
    eh, el = split(xt_ref[...])
    sign = jnp.where(lax.broadcasted_iota(jnp.int32, (1, 512), 1) % 2 == 0, -NORM, NORM)
    eh, el = split(dot3(eh, el, fx[0], fx[1]) * sign)
    for t in range(3):
        rows = slice(256 * t, 256 * t + 256)
        zh, zl = split(zt[rows, :])
        khat[rows, :] = dot3(zh, zl, eh, el)

    mine.wait()
    for when, relay in steps:
        pl.when(jnp.logical_not(relays_first) & when)(relay)

    def add_block(ahead):
        if ahead == 0:
            arrived(rows_of(0, other, 0, 128), 12 * PARTS)
        for part in range(PARTS if ahead else 0):
            for which in (0, 1):
                arrived(rows_of(ahead, which, *(far_rows if ahead == 1 else high_rows)), landing(ahead, which, part))
                if ahead == 2:
                    arrived(rows_of(2, which, *low_rows), landing(3, which, part))
        bh, bl = split(win[256 * ahead : 256 * ahead + 256, :])
        for t in range(3):
            rows, cols = slice(256 * t, 256 * t + 256), slice(256 * ahead, 256 * ahead + 256)
            part = dot3(fz[0, rows, cols], fz[1, rows, cols], bh, bl)
            acc[rows, :] = part if ahead == 0 else acc[rows, :] + part

    add_block(0)
    pl.when(gets_one)(functools.partial(add_block, 1))
    pl.when(gets_two)(functools.partial(add_block, 2))

    for t in range(3):
        rows = slice(256 * t, 256 * t + 256)
        ah, al = split(acc[rows, :])
        d = dot3(ah, al, fx[0], fx[1])
        k = khat[rows, :]
        d0, d1, d2, d3 = d[:128, :256], d[128:, :256], d[:128, 256:], d[128:, 256:]
        k0, k1, k2, k3 = k[:128, 256:], k[128:, 256:], k[:128, :256], k[128:, :256]
        for r, c, value in (
            (0, 0, d0 * k0 + d1 * k1 - d2 * k2 - d3 * k3),
            (128, 0, d1 * k0 - d0 * k1 + d2 * k3 - d3 * k2),
            (0, 256, d0 * k2 + d2 * k0 + d1 * k3 + d3 * k1),
            (128, 256, d3 * k0 - d0 * k3 + d1 * k2 - d2 * k1),
        ):
            high, low = split(value)
            what[0, 256 * t + r : 256 * t + r + 128, c : c + 256] = high
            what[1, 256 * t + r : 256 * t + r + 128, c : c + 256] = low

    own_from, own_to = pl.multiple_of(128 * other, 128), pl.multiple_of(128 * core, 128)
    across = pltpu.make_async_remote_copy(
        src_ref=wake.at[pl.ds(pl.multiple_of(128 * other, 128), 128), pl.ds(own_from, 384)],
        dst_ref=sib, send_sem=essem.at[2], recv_sem=ersem.at[2],
        device_id=at(row, other, gx), device_id_type=MESH,
    )
    gives = []
    for r in (0, 1):
        rows = slice(128 * r, 128 * r + 128)
        yh, yl = split(dot3(iz[0, rows, :], iz[1, rows, :], what[0], what[1]))
        wake[rows, :] = dot3(yh, yl, ix[0], ix[1])
        give = pltpu.make_async_remote_copy(
            src_ref=wake.at[pl.ds(128 * r, 128), pl.ds(pl.multiple_of(384 * core, 128), 128)],
            dst_ref=edge.at[other], send_sem=essem.at[r], recv_sem=ersem.at[other],
            device_id=at(row, r, gx + step), device_id_type=MESH,
        )
        pl.when(gives_edge)(give.start)
        pl.when(other == r)(across.start)
        gives.append((give, gives_edge))
    rows = pl.ds(pl.multiple_of(128 * core, 128), 128)
    out[:, pl.ds(pl.multiple_of(384 * other, 128), 128)] = jnp.zeros((128, 128), F32)
    out[:, pl.ds(own_to, 384)] = wake[rows, pl.ds(own_from, 384)]
    across.wait_recv()
    their = pl.ds(pl.multiple_of(128 * other, 128), 384)
    out[:, their] = out[:, their] + sib[...]

    def add_edge(side):
        here = edge.at[side]
        pltpu.make_async_remote_copy(
            src_ref=here, dst_ref=here, send_sem=essem.at[0], recv_sem=ersem.at[side],
            device_id=at(row, other, gx), device_id_type=MESH,
        ).wait_recv()
        there = slice(0, 128) if side == 0 else slice(384, 512)
        out[:, there] = out[:, there] + edge[side]

    pl.when(gx > 0)(functools.partial(add_edge, 0))
    pl.when(gx < 7)(functools.partial(add_edge, 1))
    sib_send.wait_send()
    across.wait_send()
    for copy, when in sends + passed + gives:
        pl.when(when)(copy.wait_send)


def local(mats, density, ztaps, xtaps):
    hbm, vmem = pl.BlockSpec(memory_space=pltpu.HBM), pl.BlockSpec(memory_space=pltpu.VMEM)
    return pl.pallas_call(
        kernel,
        out_shape=jax.ShapeDtypeStruct(density.shape, F32),
        in_specs=[hbm] * 7,
        out_specs=vmem,
        scratch_shapes=[
            pltpu.VMEM((LZ, 256), F32),
            pltpu.VMEM((2, PARTS, 128 - CUT, 256), F32),
            pltpu.VMEM((2, PARTS, 128 - TURN, 256), F32),
            pltpu.VMEM(ztaps.shape, F32),
            pltpu.VMEM(xtaps.shape, F32),
            *[pltpu.VMEM(m.shape, BF16) for m in mats],
            pltpu.VMEM((LZ, 256), F32),
            pltpu.VMEM((LZ, LX), F32),
            pltpu.VMEM((LZ, 32), F32),
            pltpu.VMEM((2, LZ, LX), BF16),
            pltpu.VMEM((256, LX), F32),
            pltpu.VMEM((128, 384), F32),
            pltpu.VMEM((2, 128, 128), F32),
            pltpu.SemaphoreType.DMA((7,)),
            pltpu.SemaphoreType.DMA((16 * PARTS,)),
            pltpu.SemaphoreType.DMA((12 * PARTS + 1,)),
            pltpu.SemaphoreType.DMA((3,)),
            pltpu.SemaphoreType.DMA((3,)),
        ],
        compiler_params=pltpu.CompilerParams(
            collective_id=0, has_side_effects=True, vmem_limit_bytes=56 * 2**20
        ),
    )(density, ztaps, xtaps, *mats)


def solution(mesh):
    mats = [jnp.asarray(m) for m in constants()]
    return jax.shard_map(
        lambda *args: local(mats, *args),
        mesh=mesh,
        in_specs=(P("gz", "gx"), P(), P()),
        out_specs=P("gz", "gx"),
        check_vma=False,
    )
```
